1024 devices in a mesh: row: 64 (over y_hi, z), col: 16 (over x, y_lo, core).
Axes of the slice: x: 4, y: 4 (y_hi: 2, y_lo: 2; y = y_hi * 2 + y_lo), z: 32, core: 2. Of those that a mesh axis runs over, the one named last changes fastest.
Arguments:
- trailing_inverse: bfloat16 [16384, 16384], P('row', 'col'), may hold values from -0.046875 to 0.046875
- l_panel: bfloat16 [16384, 512], P('row', 'col'), may hold values from -6 to 6
- pattern: int32 [64, 2], replicated, may hold values 0 or 1
Outputs:
- inverse_panel: float32 [16384, 512], P('row', 'col')
The draws below stay inside these ranges and needn't reach their ends.
Inputs may be any that keep to these rules, and one draw needn't show every extreme that they name: pattern holds only 0 and 1.
All inputs are finite; a program needn't handle non-finite values.
Results may differ from the reference program's by a relative error of at most 0.0003.
Values may be sent and summed in bfloat16 or wider, within the bound.
No kernel may reach another device: no remote copies, remote signals or barrier semaphores. Data moves between devices by JAX's collectives and lax.ppermute only.
A program may use at most 32 MiB of HBM per device.

```python
import jax
import jax.numpy as jnp

B = 256
KS = 2
R = 64


def with_ends(values, stream_key, least, largest):
    place = [jax.random.randint(jax.random.fold_in(stream_key, axis), (), 0, length) for axis, length in enumerate(values.shape)]
    widest = values.shape.index(max(values.shape))
    next_to = place[:widest] + [(place[widest] + 1) % values.shape[widest]] + place[widest + 1:]
    return values.at[tuple(place)].set(least).at[tuple(next_to)].set(largest)


def shard_levels(rng, shape, shards, smallest, high):
    factor_of = 1.0
    for dim, shards_of in shards:
        heights = jax.random.uniform(jax.random.fold_in(jax.random.fold_in(rng, 6), dim), (shards_of,), jnp.float32, smallest / len(shards), high / len(shards))
        factor_of = factor_of * jnp.repeat(jnp.exp(heights), shape[dim] // shards_of).reshape((-1,) + (1,) * (len(shape) - 1 - dim))
    return factor_of


def normal_values(key, extent, width, limit, cuts=(), dtype=jnp.bfloat16):
    drawn = width * jax.random.normal(key, extent, jnp.float32)
    if cuts:
        drawn = drawn * shard_levels(key, extent, cuts, -0.22, 0.18)
    return jnp.clip(drawn, -limit, limit).astype(dtype)


def setup_inputs(seed: int = 0) -> dict:
    splits = jax.random.split(jax.random.key(seed), 4)
    trailing_inverse = normal_values(splits[0], (R * B, R * B), (R * B) ** -0.5, 0.046875, ((0, 64), (1, 16)))
    l_panel = normal_values(splits[1], (R * B, KS * B), 1.0, 6.0, ((0, 64), (1, 16)))
    pattern = with_ends((jax.random.randint(splits[2], (R, KS), 0, 2) < 1).astype(jnp.int32), jax.random.fold_in(splits[2], 1), 0, 1)
    return dict(trailing_inverse=trailing_inverse, l_panel=l_panel, pattern=pattern)


def reference(trailing_inverse, l_panel, pattern):
    block_rows, supernodes = pattern.shape
    keep = pattern.astype(jnp.bfloat16)
    masked_panel = (l_panel.reshape(block_rows, B, supernodes, B) * keep[:, None, :, None]).reshape(block_rows * B, supernodes * B)
    product = jnp.dot(trailing_inverse, masked_panel, preferred_element_type=jnp.float32)
    negated = -pattern.astype(jnp.float32)
    result = product.reshape(block_rows, B, supernodes, B) * negated[:, None, :, None]
    return result.reshape(block_rows * B, supernodes * B)
```

```python
import jax
import jax.numpy as jnp
from jax import lax
from jax.experimental import pallas as pl
from jax.experimental.pallas import tpu as pltpu
from jax.sharding import Mesh, PartitionSpec as P

ROWS = ("half", "slab", "plane", "twin")
COLS = ("x", "y", "core")
QUAD = ("y", "core")


def product(panel_ref, inverse_ref, out_ref):
    halves, twins, quads, planes, pairs, width, order = panel_ref.shape
    total = jnp.zeros(out_ref.shape, jnp.float32)
    for half in range(halves):
        for pair in range(pairs):
            for plane in range(planes * twins):
                left = panel_ref[half, plane % twins, :, plane // twins, pair].reshape(quads * width, order)
                right = inverse_ref[half * pairs + pair, :, plane * order:(plane + 1) * order]
                total += lax.dot_general(left, right, (((1,), (1,)), ((), ())), preferred_element_type=jnp.float32)
    out_ref[...] = total


def multiply(panel, inverse):
    halves, twins, quads, planes, pairs, width, order = panel.shape
    vmem = pl.BlockSpec(memory_space=pltpu.VMEM)
    return pl.pallas_call(
        product,
        in_specs=[vmem, vmem],
        out_specs=vmem,
        out_shape=jax.ShapeDtypeStruct((quads * width, order), jnp.float32),
        cost_estimate=pl.CostEstimate(
            flops=2 * panel.size * order, bytes_accessed=2 * (panel.size + inverse.size), transcendentals=0
        ),
        compiler_params=pltpu.CompilerParams(vmem_limit_bytes=16 * 1024 * 1024),
    )(panel, inverse)


def per_device(trailing_inverse, l_panel, pattern):
    half, twin = lax.axis_index("half"), lax.axis_index("twin")
    row, col = lax.axis_index(ROWS), lax.axis_index(COLS)
    halves, slabs, planes, twins = (lax.axis_size(a) for a in ROWS)
    cols, quads = lax.axis_size(COLS), lax.axis_size(QUAD)
    pairs = slabs // quads
    order, width = l_panel.shape
    supernode = col * pattern.shape[1] // cols
    copies = jnp.broadcast_to(trailing_inverse[None], (lax.axis_size("x"),) + trailing_inverse.shape)
    inverse = lax.all_to_all(copies, "x", 0, 0)
    gathered = lax.all_gather(l_panel.T, ("slab", "plane"), axis=0)
    gathered = gathered.reshape(pairs, quads, planes, width, order)
    flags = lax.dynamic_index_in_dim(pattern, supernode, 1, keepdims=False)
    flags = flags.reshape(halves, pairs, quads, planes, twins)[half, ..., twin]
    masked = gathered * flags[..., None, None].astype(gathered.dtype)
    masked = masked.transpose(1, 2, 0, 3, 4)
    chunks = jnp.broadcast_to(masked[None], (halves * twins,) + masked.shape)
    panel = lax.all_to_all(chunks.reshape((-1,) + masked.shape[1:]), ("half", "twin") + QUAD, 0, 0)
    panel = panel.reshape((halves, twins) + masked.shape)
    partial = multiply(panel, inverse)
    shares = lax.all_to_all(partial.reshape(quads, width, order), QUAD, 0, 0)
    mine = pattern[row, supernode]
    return (jnp.sum(shares, 0) * -mine.astype(jnp.float32)).T


def solution(mesh):
    devices = mesh.devices.reshape(2, 8, 2, 2, 4, 2, 2)
    fine = Mesh(devices, ROWS + COLS)
    return jax.shard_map(
        per_device,
        mesh=fine,
        in_specs=(P(ROWS, COLS), P(ROWS, COLS), P()),
        out_specs=P(ROWS, COLS),
        check_vma=False,
    )
```

```python
import jax
import jax.numpy as jnp
from jax import lax
from jax.experimental import pallas as pl
from jax.experimental.pallas import tpu as pltpu
from jax.sharding import Mesh, PartitionSpec as P

ROWS = ("half", "slab", "plane", "twin")
COLS = ("x", "y", "core")
QUAD = ("y", "core")


def product(panel_ref, inverse_ref, out_ref):
    halves, twins, quads, planes, pairs, width, order = panel_ref.shape
    total = jnp.zeros(out_ref.shape[::-1], jnp.float32)
    for half in range(halves):
        for pair in range(pairs):
            for plane in range(planes * twins):
                left = panel_ref[half, plane % twins, :, plane // twins, pair].reshape(quads * width, order)
                right = inverse_ref[half * pairs + pair, :, plane * order:(plane + 1) * order]
                total += lax.dot_general(right, left, (((1,), (1,)), ((), ())), preferred_element_type=jnp.float32)
    out_ref[...] = total.T


def multiply(panel, inverse):
    halves, twins, quads, planes, pairs, width, order = panel.shape
    vmem = pl.BlockSpec(memory_space=pltpu.VMEM)
    return pl.pallas_call(
        product,
        in_specs=[vmem, vmem],
        out_specs=vmem,
        out_shape=jax.ShapeDtypeStruct((quads * width, order), jnp.float32),
        cost_estimate=pl.CostEstimate(
            flops=2 * panel.size * order, bytes_accessed=2 * (panel.size + inverse.size), transcendentals=0
        ),
        compiler_params=pltpu.CompilerParams(vmem_limit_bytes=16 * 1024 * 1024),
    )(panel, inverse)


def copy_out(value_ref, out_ref, held_ref, load_sems, store_sems):
    parts, count = load_sems.shape[0], out_ref.shape[0]
    depth = value_ref.shape[0] // parts
    spans = [pl.ds(i * depth, depth) for i in range(parts)]
    loads = [pltpu.make_async_copy(value_ref.at[s], held_ref.at[s], load_sems.at[i]) for i, s in enumerate(spans)]
    stores = [
        [pltpu.make_async_copy(held_ref.at[s], out_ref.at[j, s], store_sems.at[i, j]) for j in range(count)]
        for i, s in enumerate(spans)
    ]
    for load in loads:
        load.start()
    for load, group in zip(loads, stores):
        load.wait()
        for store in group:
            store.start()
    for group in stores:
        for store in group:
            store.wait()


def repeat(value, count):
    parts = 2
    return pl.pallas_call(
        copy_out,
        in_specs=[pl.BlockSpec(memory_space=pl.ANY)],
        out_specs=pl.BlockSpec(memory_space=pl.ANY),
        out_shape=jax.ShapeDtypeStruct((count,) + value.shape, value.dtype),
        scratch_shapes=[
            pltpu.VMEM(value.shape, value.dtype),
            pltpu.SemaphoreType.DMA((parts,)),
            pltpu.SemaphoreType.DMA((parts, count)),
        ],
    )(value)


def per_device(trailing_inverse, l_panel, pattern):
    half, plane, twin = lax.axis_index("half"), lax.axis_index("plane"), lax.axis_index("twin")
    row, col = lax.axis_index(ROWS), lax.axis_index(COLS)
    halves, slabs, planes, twins = (lax.axis_size(a) for a in ROWS)
    cols, quads = lax.axis_size(COLS), lax.axis_size(QUAD)
    core, cores, ys = lax.axis_index("core"), lax.axis_size("core"), lax.axis_size("y")
    pairs = slabs // quads
    order, width = l_panel.shape
    supernode = col * pattern.shape[1] // cols
    copies = repeat(trailing_inverse, lax.axis_size("x"))
    piece = l_panel.T
    facing = lax.ppermute(piece, "plane", [(0, 1), (1, 0)])
    copies, facing = lax.optimization_barrier((copies, facing))
    inverse = lax.all_to_all(copies, "x", 0, 0)
    couple = jnp.where(plane == 0, jnp.stack([piece, facing]), jnp.stack([facing, piece]))
    gathered = lax.all_gather(couple, ("slab", "core"), axis=0)
    gathered = gathered.reshape(pairs, ys, cores, cores, planes, width, order)
    gathered = lax.dynamic_index_in_dim(gathered, core, 2, keepdims=False)
    flags = lax.dynamic_index_in_dim(pattern, supernode, 1, keepdims=False)
    flags = flags.reshape(halves, pairs, ys, cores, planes, twins)[half, :, :, core, :, twin]
    masked = gathered * flags[:, :, None, :, None, None].astype(gathered.dtype)
    masked = masked.transpose(1, 2, 3, 0, 4, 5)
    chunks = jnp.broadcast_to(masked[None], (halves * twins,) + masked.shape)
    panel = lax.all_to_all(chunks.reshape((-1,) + masked.shape[1:]), ("half", "twin", "y"), 0, 0)
    panel = panel.reshape((halves, twins, quads) + masked.shape[2:])
    partial = multiply(panel, inverse)
    shares = lax.all_to_all(partial.reshape(quads, width, order), QUAD, 0, 0)
    mine = pattern[row, supernode]
    return (jnp.sum(shares, 0) * -mine.astype(jnp.float32)).T


def solution(mesh):
    devices = mesh.devices.reshape(2, 8, 2, 2, 4, 2, 2)
    fine = Mesh(devices, ROWS + COLS)
    return jax.shard_map(
        per_device,
        mesh=fine,
        in_specs=(P(ROWS, COLS), P(ROWS, COLS), P()),
        out_specs=P(ROWS, COLS),
        check_vma=False,
    )
```

```python
import jax
import jax.numpy as jnp
from jax import lax
from jax.experimental import pallas as pl
from jax.experimental.pallas import tpu as pltpu
from jax.sharding import Mesh, PartitionSpec as P

ROWS = ("half", "slab", "plane", "twin")
COLS = ("x", "y", "core")
QUAD = ("y", "core")


def product(pattern_ref, panel_ref, inverse_ref, out_ref):
    halves, twins, quads, planes, pairs, width, order = panel_ref.shape
    supernodes, cols = pattern_ref.shape[0], lax.axis_size(COLS)
    supernode, quad = lax.axis_index(COLS) * supernodes // cols, lax.axis_index(QUAD)
    total = jnp.zeros(out_ref.shape[::-1], jnp.float32)
    for half in range(halves):
        for pair in range(pairs):
            slab = (half * pairs + pair) * quads + quad
            for plane in range(planes):
                for twin in range(twins):
                    step = plane * twins + twin
                    keep = pattern_ref[supernode, slab * planes * twins + step]
                    left = panel_ref[half, twin, :, plane, pair].reshape(quads * width, order)
                    left = jnp.where(keep != 0, left, jnp.zeros_like(left))
                    right = inverse_ref[half * pairs + pair, :, step * order:(step + 1) * order]
                    total += lax.dot_general(right, left, (((1,), (1,)), ((), ())), preferred_element_type=jnp.float32)
    mine = pattern_ref[supernode, lax.axis_index(ROWS)]
    out_ref[...] = total.T * -mine.astype(jnp.float32)


def multiply(pattern, panel, inverse):
    halves, twins, quads, planes, pairs, width, order = panel.shape
    vmem = pl.BlockSpec(memory_space=pltpu.VMEM)
    return pl.pallas_call(
        product,
        in_specs=[pl.BlockSpec(memory_space=pltpu.SMEM), vmem, vmem],
        out_specs=vmem,
        out_shape=jax.ShapeDtypeStruct((quads * width, order), jnp.float32),
        cost_estimate=pl.CostEstimate(
            flops=2 * panel.size * order, bytes_accessed=2 * (panel.size + inverse.size), transcendentals=0
        ),
        compiler_params=pltpu.CompilerParams(vmem_limit_bytes=16 * 1024 * 1024),
    )(pattern.T, panel, inverse)


def copy_out(value_ref, out_ref, held_ref, load_sems, store_sems):
    parts, count = load_sems.shape[0], out_ref.shape[0]
    depth = value_ref.shape[0] // parts
    spans = [pl.ds(i * depth, depth) for i in range(parts)]
    loads = [pltpu.make_async_copy(value_ref.at[s], held_ref.at[s], load_sems.at[i]) for i, s in enumerate(spans)]
    stores = [
        [pltpu.make_async_copy(held_ref.at[s], out_ref.at[j, s], store_sems.at[i, j]) for j in range(count)]
        for i, s in enumerate(spans)
    ]
    for load in loads:
        load.start()
    for load, group in zip(loads, stores):
        load.wait()
        for store in group:
            store.start()
    for group in stores:
        for store in group:
            store.wait()


def repeat(value, count):
    parts = 2
    return pl.pallas_call(
        copy_out,
        in_specs=[pl.BlockSpec(memory_space=pl.ANY)],
        out_specs=pl.BlockSpec(memory_space=pl.ANY),
        out_shape=jax.ShapeDtypeStruct((count,) + value.shape, value.dtype),
        scratch_shapes=[
            pltpu.VMEM(value.shape, value.dtype),
            pltpu.SemaphoreType.DMA((parts,)),
            pltpu.SemaphoreType.DMA((parts, count)),
        ],
    )(value)


def per_device(trailing_inverse, l_panel, pattern):
    plane = lax.axis_index("plane")
    halves, slabs, planes, twins = (lax.axis_size(a) for a in ROWS)
    quads = lax.axis_size(QUAD)
    core, cores, ys = lax.axis_index("core"), lax.axis_size("core"), lax.axis_size("y")
    pairs = slabs // quads
    order, width = l_panel.shape
    copies = repeat(trailing_inverse, lax.axis_size("x"))
    piece = l_panel.T
    facing = lax.ppermute(piece, "plane", [(0, 1), (1, 0)])
    copies, facing = lax.optimization_barrier((copies, facing))
    inverse = lax.all_to_all(copies, "x", 0, 0)
    couple = jnp.where(plane == 0, jnp.stack([piece, facing]), jnp.stack([facing, piece]))
    gathered = lax.all_gather(couple, ("slab", "core"), axis=0)
    gathered = gathered.reshape(pairs, ys, cores, cores, planes, width, order)
    gathered = lax.dynamic_index_in_dim(gathered, core, 2, keepdims=False)
    pieces = gathered.transpose(1, 2, 3, 0, 4, 5)
    chunks = jnp.broadcast_to(pieces[None], (halves * twins,) + pieces.shape)
    panel = lax.all_to_all(chunks.reshape((-1,) + pieces.shape[1:]), ("half", "twin", "y"), 0, 0)
    panel = panel.reshape((halves, twins, quads) + pieces.shape[2:])
    partial = multiply(pattern, panel, inverse)
    shares = lax.all_to_all(partial.reshape(quads, width, order), QUAD, 0, 0)
    return jnp.sum(shares, 0).T


def solution(mesh):
    devices = mesh.devices.reshape(2, 8, 2, 2, 4, 2, 2)
    fine = Mesh(devices, ROWS + COLS)
    return jax.shard_map(
        per_device,
        mesh=fine,
        in_specs=(P(ROWS, COLS), P(ROWS, COLS), P()),
        out_specs=P(ROWS, COLS),
        check_vma=False,
    )
```

```python
import jax
import jax.numpy as jnp
from jax import lax
from jax.experimental import pallas as pl
from jax.experimental.pallas import tpu as pltpu
from jax.sharding import Mesh, PartitionSpec as P

ROWS = ("half", "slab", "plane", "twin")
COLS = ("x", "y", "core")
QUAD = ("y", "core")
SHARE = ("twin", "y", "half")


def product(pattern_ref, panel_ref, inverse_ref, out_ref):
    sizes = dict(zip(SHARE, panel_ref.shape))
    halves, twins, ys = sizes["half"], sizes["twin"], sizes["y"]
    cores, planes, pairs, width, order = panel_ref.shape[3:]
    quads = ys * cores
    supernodes, cols = pattern_ref.shape[0], lax.axis_size(COLS)
    supernode, quad = lax.axis_index(COLS) * supernodes // cols, lax.axis_index(QUAD)
    total = jnp.zeros(out_ref.shape[::-1], jnp.float32)
    for half in range(halves):
        for pair in range(pairs):
            slab = (half * pairs + pair) * quads + quad
            for plane in range(planes):
                for twin in range(twins):
                    step = plane * twins + twin
                    keep = pattern_ref[supernode, slab * planes * twins + step]
                    places = [dict(half=half, twin=twin, y=y) for y in range(ys)]
                    parts = [panel_ref[tuple(p[a] for a in SHARE) + (slice(None), plane, pair)] for p in places]
                    left = jnp.concatenate([p.reshape(cores * width, order) for p in parts])
                    left = jnp.where(keep != 0, left, jnp.zeros_like(left))
                    right = inverse_ref[half * pairs + pair, :, step * order:(step + 1) * order]
                    total += lax.dot_general(right, left, (((1,), (1,)), ((), ())), preferred_element_type=jnp.float32)
    mine = pattern_ref[supernode, lax.axis_index(ROWS)]
    out_ref[...] = total.T * -mine.astype(jnp.float32)


def multiply(pattern, panel, inverse):
    width, order = panel.shape[-2:]
    quads = lax.axis_size(QUAD)
    vmem = pl.BlockSpec(memory_space=pltpu.VMEM)
    return pl.pallas_call(
        product,
        in_specs=[pl.BlockSpec(memory_space=pltpu.SMEM), vmem, vmem],
        out_specs=vmem,
        out_shape=jax.ShapeDtypeStruct((quads * width, order), jnp.float32),
        cost_estimate=pl.CostEstimate(
            flops=2 * panel.size * order, bytes_accessed=2 * (panel.size + inverse.size), transcendentals=0
        ),
        compiler_params=pltpu.CompilerParams(vmem_limit_bytes=16 * 1024 * 1024),
    )(pattern.T, panel, inverse)


def copy_out(value_ref, out_ref, held_ref, load_sems, store_sems):
    parts, count = load_sems.shape[0], out_ref.shape[0]
    depth = value_ref.shape[0] // parts
    spans = [pl.ds(i * depth, depth) for i in range(parts)]
    loads = [pltpu.make_async_copy(value_ref.at[s], held_ref.at[s], load_sems.at[i]) for i, s in enumerate(spans)]
    stores = [
        [pltpu.make_async_copy(held_ref.at[s], out_ref.at[j, s], store_sems.at[i, j]) for j in range(count)]
        for i, s in enumerate(spans)
    ]
    for load in loads:
        load.start()
    for load, group in zip(loads, stores):
        load.wait()
        for store in group:
            store.start()
    for group in stores:
        for store in group:
            store.wait()


def repeat(value, count):
    parts = 2
    return pl.pallas_call(
        copy_out,
        in_specs=[pl.BlockSpec(memory_space=pl.ANY)],
        out_specs=pl.BlockSpec(memory_space=pl.ANY),
        out_shape=jax.ShapeDtypeStruct((count,) + value.shape, value.dtype),
        scratch_shapes=[
            pltpu.VMEM(value.shape, value.dtype),
            pltpu.SemaphoreType.DMA((parts,)),
            pltpu.SemaphoreType.DMA((parts, count)),
        ],
    )(value)


def per_device(trailing_inverse, l_panel, pattern):
    plane = lax.axis_index("plane")
    halves, slabs, planes, twins = (lax.axis_size(a) for a in ROWS)
    quads = lax.axis_size(QUAD)
    core, cores, ys = lax.axis_index("core"), lax.axis_size("core"), lax.axis_size("y")
    pairs = slabs // quads
    order, width = l_panel.shape
    copies = repeat(trailing_inverse, lax.axis_size("x"))
    piece = l_panel.T
    facing = lax.ppermute(piece, "plane", [(0, 1), (1, 0)])
    copies, facing = lax.optimization_barrier((copies, facing))
    inverse = lax.all_to_all(copies, "x", 0, 0)
    couple = jnp.where(plane == 0, jnp.stack([piece, facing]), jnp.stack([facing, piece]))
    gathered = lax.all_gather(couple, ("slab", "core"), axis=0)
    gathered = gathered.reshape(pairs, ys, cores, cores, planes, width, order)
    gathered = lax.dynamic_index_in_dim(gathered, core, 2, keepdims=False)
    pieces = gathered.transpose(1, 2, 3, 0, 4, 5)
    sizes = tuple(lax.axis_size(a) for a in SHARE)
    chunks = jnp.broadcast_to(jnp.expand_dims(pieces, [i for i, a in enumerate(SHARE) if a != "y"]), sizes + pieces.shape[1:])
    panel = lax.all_to_all(chunks.reshape((-1,) + pieces.shape[1:]), SHARE, 0, 0)
    panel = panel.reshape(sizes + pieces.shape[1:])
    partial = multiply(pattern, panel, inverse)
    shares = lax.all_to_all(partial.reshape(quads, width, order), QUAD, 0, 0)
    return jnp.sum(shares, 0).T


def solution(mesh):
    devices = mesh.devices.reshape(2, 8, 2, 2, 4, 2, 2)
    fine = Mesh(devices, ROWS + COLS)
    return jax.shard_map(
        per_device,
        mesh=fine,
        in_specs=(P(ROWS, COLS), P(ROWS, COLS), P()),
        out_specs=P(ROWS, COLS),
        check_vma=False,
    )
```

```python
import jax
import jax.numpy as jnp
from jax import lax
from jax.experimental import pallas as pl
from jax.experimental.pallas import tpu as pltpu
from jax.sharding import Mesh, PartitionSpec as P

ROWS = ("half", "slab", "plane", "twin")
COLS = ("x", "y", "core")
QUAD = ("y", "core")
SHARE = ("twin", "y", "half")


def product(pattern_ref, panel_ref, inverse_ref, out_ref):
    sizes = dict(zip(SHARE, panel_ref.shape))
    halves, twins, ys = sizes["half"], sizes["twin"], sizes["y"]
    cores, planes, pairs, width, order = panel_ref.shape[3:]
    quads = ys * cores
    supernodes, cols = pattern_ref.shape[0], lax.axis_size(COLS)
    supernode, quad = lax.axis_index(COLS) * supernodes // cols, lax.axis_index(QUAD)
    factors = jnp.where(supernode == 0, pattern_ref[0:1], pattern_ref[1:2])
    lanes = lax.broadcasted_iota(jnp.int32, factors.shape, 1)
    total = jnp.zeros(out_ref.shape[::-1], jnp.float32)
    for half in range(halves):
        for pair in range(pairs):
            slab = (half * pairs + pair) * quads + quad
            for plane in range(planes):
                for twin in range(twins):
                    step = plane * twins + twin
                    keep = jnp.sum(jnp.where(lanes == slab * planes * twins + step, factors, 0), axis=1, keepdims=True)
                    places = [dict(half=half, twin=twin, y=y) for y in range(ys)]
                    parts = [panel_ref[tuple(p[a] for a in SHARE) + (slice(None), plane, pair)] for p in places]
                    left = jnp.concatenate([p.reshape(cores * width, order) for p in parts])
                    left = left * keep.astype(left.dtype)
                    right = inverse_ref[half * pairs + pair, :, step * order:(step + 1) * order]
                    total += lax.dot_general(right, left, (((1,), (1,)), ((), ())), preferred_element_type=jnp.float32)
    mine = jnp.sum(jnp.where(lanes == lax.axis_index(ROWS), factors, 0), axis=1, keepdims=True)
    out_ref[...] = total.T * -mine.astype(jnp.float32)


def multiply(pattern, panel, inverse):
    width, order = panel.shape[-2:]
    quads = lax.axis_size(QUAD)
    vmem = pl.BlockSpec(memory_space=pltpu.VMEM)
    return pl.pallas_call(
        product,
        in_specs=[vmem, vmem, vmem],
        out_specs=vmem,
        out_shape=jax.ShapeDtypeStruct((quads * width, order), jnp.float32),
        cost_estimate=pl.CostEstimate(
            flops=2 * panel.size * order, bytes_accessed=2 * (panel.size + inverse.size), transcendentals=0
        ),
        compiler_params=pltpu.CompilerParams(vmem_limit_bytes=16 * 1024 * 1024),
    )(pattern.T, panel, inverse)


def copy_out(value_ref, out_ref, held_ref, load_sems, store_sems):
    parts, count = load_sems.shape[0], out_ref.shape[0]
    depth = value_ref.shape[0] // parts
    spans = [pl.ds(i * depth, depth) for i in range(parts)]
    loads = [pltpu.make_async_copy(value_ref.at[s], held_ref.at[s], load_sems.at[i]) for i, s in enumerate(spans)]
    stores = [
        [pltpu.make_async_copy(held_ref.at[s], out_ref.at[j, s], store_sems.at[i, j]) for j in range(count)]
        for i, s in enumerate(spans)
    ]
    for load in loads:
        load.start()
    for load, group in zip(loads, stores):
        load.wait()
        for store in group:
            store.start()
    for group in stores:
        for store in group:
            store.wait()


def repeat(value, count):
    parts = 2
    return pl.pallas_call(
        copy_out,
        in_specs=[pl.BlockSpec(memory_space=pl.ANY)],
        out_specs=pl.BlockSpec(memory_space=pl.ANY),
        out_shape=jax.ShapeDtypeStruct((count,) + value.shape, value.dtype),
        scratch_shapes=[
            pltpu.VMEM(value.shape, value.dtype),
            pltpu.SemaphoreType.DMA((parts,)),
            pltpu.SemaphoreType.DMA((parts, count)),
        ],
    )(value)


def per_device(trailing_inverse, l_panel, pattern):
    plane = lax.axis_index("plane")
    halves, slabs, planes, twins = (lax.axis_size(a) for a in ROWS)
    quads = lax.axis_size(QUAD)
    core, cores, ys = lax.axis_index("core"), lax.axis_size("core"), lax.axis_size("y")
    pairs = slabs // quads
    order, width = l_panel.shape
    copies = repeat(trailing_inverse, lax.axis_size("x"))
    piece = l_panel.T
    facing = lax.ppermute(piece, "plane", [(0, 1), (1, 0)])
    copies, facing = lax.optimization_barrier((copies, facing))
    inverse = lax.all_to_all(copies, "x", 0, 0)
    couple = jnp.where(plane == 0, jnp.stack([piece, facing]), jnp.stack([facing, piece]))
    gathered = lax.all_gather(couple, ("slab", "core"), axis=0)
    gathered = gathered.reshape(pairs, ys, cores, cores, planes, width, order)
    gathered = lax.dynamic_index_in_dim(gathered, core, 2, keepdims=False)
    pieces = gathered.transpose(1, 2, 3, 0, 4, 5)
    sizes = tuple(lax.axis_size(a) for a in SHARE)
    chunks = jnp.broadcast_to(jnp.expand_dims(pieces, [i for i, a in enumerate(SHARE) if a != "y"]), sizes + pieces.shape[1:])
    panel = lax.all_to_all(chunks.reshape((-1,) + pieces.shape[1:]), SHARE, 0, 0)
    panel = panel.reshape(sizes + pieces.shape[1:])
    partial = multiply(pattern, panel, inverse)
    shares = lax.all_to_all(partial.reshape(quads, width, order), QUAD, 0, 0)
    return jnp.sum(shares, 0).T


def solution(mesh):
    devices = mesh.devices.reshape(2, 8, 2, 2, 4, 2, 2)
    fine = Mesh(devices, ROWS + COLS)
    return jax.shard_map(
        per_device,
        mesh=fine,
        in_specs=(P(ROWS, COLS), P(ROWS, COLS), P()),
        out_specs=P(ROWS, COLS),
        check_vma=False,
    )
```

```python
import jax
import jax.numpy as jnp
from jax import lax
from jax.experimental import pallas as pl
from jax.experimental.pallas import tpu as pltpu
from jax.sharding import Mesh, PartitionSpec as P

ROWS = ("half", "slab", "plane", "twin")
COLS = ("x", "y", "core")
QUAD = ("y", "core")
SHARE = ("twin", "y", "half")


def product(pattern_ref, panel_ref, inverse_ref, out_ref):
    sizes = dict(zip(SHARE, panel_ref.shape))
    halves, twins, ys = sizes["half"], sizes["twin"], sizes["y"]
    cores, planes, pairs, width, order = panel_ref.shape[3:]
    quads = ys * cores
    supernodes, cols = pattern_ref.shape[0], lax.axis_size(COLS)
    supernode, quad = lax.axis_index(COLS) * supernodes // cols, lax.axis_index(QUAD)
    factors = jnp.where(supernode == 0, pattern_ref[0:1], pattern_ref[1:2])
    lanes = lax.broadcasted_iota(jnp.int32, factors.shape, 1)
    total = jnp.zeros(out_ref.shape[::-1], jnp.float32)
    for half in range(halves):
        for pair in range(pairs):
            slab = (half * pairs + pair) * quads + quad
            pieces = []
            for step in range(planes * twins):
                keep = jnp.sum(jnp.where(lanes == slab * planes * twins + step, factors, 0), axis=1, keepdims=True)
                places = [dict(half=half, twin=step % twins, y=y) for y in range(ys)]
                at = (slice(None), step // twins, pair)
                parts = [panel_ref[tuple(p[a] for a in SHARE) + at].reshape(cores * width, order) for p in places]
                pieces.append(jnp.concatenate(parts) * keep.astype(panel_ref.dtype))
            left, right = jnp.concatenate(pieces, axis=1), inverse_ref[half * pairs + pair]
            total += lax.dot_general(right, left, (((1,), (1,)), ((), ())), preferred_element_type=jnp.float32)
    mine = jnp.sum(jnp.where(lanes == lax.axis_index(ROWS), factors, 0), axis=1, keepdims=True)
    out_ref[...] = total.T * -mine.astype(jnp.float32)


def multiply(pattern, panel, inverse):
    width, order = panel.shape[-2:]
    quads = lax.axis_size(QUAD)
    vmem = pl.BlockSpec(memory_space=pltpu.VMEM)
    return pl.pallas_call(
        product,
        in_specs=[vmem, vmem, vmem],
        out_specs=vmem,
        out_shape=jax.ShapeDtypeStruct((quads * width, order), jnp.float32),
        cost_estimate=pl.CostEstimate(
            flops=2 * panel.size * order, bytes_accessed=2 * (panel.size + inverse.size), transcendentals=0
        ),
        compiler_params=pltpu.CompilerParams(vmem_limit_bytes=16 * 1024 * 1024),
    )(pattern.T, panel, inverse)


def copy_out(value_ref, out_ref, held_ref, load_sems, store_sems):
    parts, count = load_sems.shape[0], out_ref.shape[0]
    depth = value_ref.shape[0] // parts
    spans = [pl.ds(i * depth, depth) for i in range(parts)]
    loads = [pltpu.make_async_copy(value_ref.at[s], held_ref.at[s], load_sems.at[i]) for i, s in enumerate(spans)]
    stores = [
        [pltpu.make_async_copy(held_ref.at[s], out_ref.at[j, s], store_sems.at[i, j]) for j in range(count)]
        for i, s in enumerate(spans)
    ]
    for load in loads:
        load.start()
    for load, group in zip(loads, stores):
        load.wait()
        for store in group:
            store.start()
    for group in stores:
        for store in group:
            store.wait()


def repeat(value, count):
    parts = 2
    return pl.pallas_call(
        copy_out,
        in_specs=[pl.BlockSpec(memory_space=pl.ANY)],
        out_specs=pl.BlockSpec(memory_space=pl.ANY),
        out_shape=jax.ShapeDtypeStruct((count,) + value.shape, value.dtype),
        scratch_shapes=[
            pltpu.VMEM(value.shape, value.dtype),
            pltpu.SemaphoreType.DMA((parts,)),
            pltpu.SemaphoreType.DMA((parts, count)),
        ],
    )(value)


def per_device(trailing_inverse, l_panel, pattern):
    plane = lax.axis_index("plane")
    halves, slabs, planes, twins = (lax.axis_size(a) for a in ROWS)
    quads = lax.axis_size(QUAD)
    core, cores, ys = lax.axis_index("core"), lax.axis_size("core"), lax.axis_size("y")
    pairs = slabs // quads
    order, width = l_panel.shape
    copies = repeat(trailing_inverse, lax.axis_size("x"))
    piece = l_panel.T
    facing = lax.ppermute(piece, "plane", [(0, 1), (1, 0)])
    copies, facing = lax.optimization_barrier((copies, facing))
    inverse = lax.all_to_all(copies, "x", 0, 0)
    couple = jnp.where(plane == 0, jnp.stack([piece, facing]), jnp.stack([facing, piece]))
    gathered = lax.all_gather(couple, ("slab", "core"), axis=0)
    gathered = gathered.reshape(pairs, ys, cores, cores, planes, width, order)
    gathered = lax.dynamic_index_in_dim(gathered, core, 2, keepdims=False)
    pieces = gathered.transpose(1, 2, 3, 0, 4, 5)
    sizes = tuple(lax.axis_size(a) for a in SHARE)
    chunks = jnp.broadcast_to(jnp.expand_dims(pieces, [i for i, a in enumerate(SHARE) if a != "y"]), sizes + pieces.shape[1:])
    panel = lax.all_to_all(chunks.reshape((-1,) + pieces.shape[1:]), SHARE, 0, 0)
    panel = panel.reshape(sizes + pieces.shape[1:])
    partial = multiply(pattern, panel, inverse)
    shares = lax.all_to_all(partial.reshape(quads, width, order), QUAD, 0, 0)
    return jnp.sum(shares, 0).T


def solution(mesh):
    devices = mesh.devices.reshape(2, 8, 2, 2, 4, 2, 2)
    fine = Mesh(devices, ROWS + COLS)
    return jax.shard_map(
        per_device,
        mesh=fine,
        in_specs=(P(ROWS, COLS), P(ROWS, COLS), P()),
        out_specs=P(ROWS, COLS),
        check_vma=False,
    )
```
